32 devices in a mesh: ctx: 4 (over y, core), head: 8 (over z, x).
Axes of the slice: x: 2, y: 2, z: 4, core: 2. Of those that a mesh axis runs over, the one named last changes fastest.
Arguments:
- conv_input: bfloat16 [8192, 20480], P(('ctx', 'head')), may hold values from -6 to 6
- dt_raw: bfloat16 [8192, 256], P(('ctx', 'head')), as said below
- conv_weight: bfloat16 [4, 20480], replicated, may hold values from -3 to 3
- conv_bias: float32 [20480], replicated, may hold values from -3 to 3
- a_log: float32 [256], replicated, may hold values from -0.2 to 0.2
- dt_bias: float32 [256], replicated, as said below
- d_skip: float32 [256], replicated, may hold values from 0.5 to 1.5
Outputs:
- scan_out: bfloat16 [8192, 16384], P('ctx', 'head')
The draws below stay inside these ranges and needn't reach their ends.
Inputs may be any that keep to these rules, and one draw needn't show every extreme that they name: softplus(dt_bias[h]) lies between 0.02 / 8192 and 0.04 for every head. softplus(dt_raw[t, h] + dt_bias[h]) lies between 0.02 / 8192 and 0.5 for every token and head.
All inputs are finite; a program needn't handle non-finite values.
Results may differ from the reference program's by a relative error of at most 0.0046.
Values may be sent and summed in bfloat16 or wider, within the bound.
A program may use at most 256 MiB of HBM per device.

```python
import jax
import jax.numpy as jnp
from jax import lax

HEADS = 256
HEADDIM = 64
STATE = 256
GROUPS = 8
CONV = 4
SPAN = 512
TOK_DEV = 256
INPUT_LENGTH = 8192
XBCW = 20480


def head_profile(key):
    first, second, third = jax.random.split(jax.random.fold_in(key, 7), 3)
    share = 0.5
    gradual_trend = jax.random.uniform(first, (HEADS,), jnp.float32) < share
    fast_step = jax.random.uniform(second, (HEADS,), jnp.float32, 0.02, 0.035)
    slow_step = jax.random.uniform(third, (HEADS,), jnp.float32, 0.1, 0.3) / INPUT_LENGTH
    constant_floor = jnp.where(gradual_trend, jnp.log(slow_step), jnp.log(fast_step))
    return (gradual_trend, constant_floor)


def draw_dt_bias(key, part):
    gradual_trend, constant_floor = head_profile(key)
    return constant_floor.astype(jnp.float32)


def draw_dt_raw(key, part):
    gradual_trend, constant_floor = head_profile(key)
    first, second, third = jax.random.split(jax.random.fold_in(key, 11), 3)
    noise_term = jnp.clip(0.5 * jax.random.normal(first, (INPUT_LENGTH, HEADS), jnp.float32), -1.2, 1.2)
    displacement_amounts = jax.random.uniform(second, (INPUT_LENGTH // TOK_DEV, HEADS), jnp.float32, -0.35, 0.35)
    displacement_amounts = jnp.repeat(displacement_amounts, TOK_DEV, axis=0)
    impulse_indices = jnp.arange(8, dtype=jnp.int32) * (INPUT_LENGTH // 8) + jax.random.randint(third, (8,), 0, INPUT_LENGTH // 8)
    impulse_height = jnp.any(jnp.arange(INPUT_LENGTH, dtype=jnp.int32)[:, None] == impulse_indices[None, :], axis=1)
    sequence_samples = jnp.where(impulse_height[:, None] & gradual_trend[None, :], -1.5 - constant_floor[None, :], noise_term + displacement_amounts)
    return sequence_samples.astype(jnp.bfloat16)


def shard_levels(key, dims, cuts, smallest, top_value):
    gain, own = 1.0, jax.random.fold_in(key, 6)
    for axis_at, shards_of in cuts:
        heights = jnp.exp(jax.random.uniform(jax.random.fold_in(own, axis_at), (shards_of,), jnp.float32, smallest / len(cuts), top_value / len(cuts)))
        gain = gain * jnp.repeat(heights, dims[axis_at] // shards_of).reshape([-1 if axis == axis_at else 1 for axis in range(len(dims))])
    return gain


def scatter_about(rng, shape, spread, reach, shards=(), held_as=jnp.bfloat16):
    array = spread * jax.random.normal(rng, shape, jnp.float32)
    if shards:
        array = array * shard_levels(rng, shape, shards, -0.22, 0.18)
    return jnp.clip(array, -reach, reach).astype(held_as)


def setup_inputs(seed: int = 0) -> dict:
    splits = jax.random.split(jax.random.key(seed), 8)
    conv_input = scatter_about(splits[0], (INPUT_LENGTH, XBCW), 1.0, 6.0, ((0, 32),))
    dt_raw = draw_dt_raw(jax.random.fold_in(splits[7], 71), 0)
    conv_weight = scatter_about(splits[2], (CONV, XBCW), CONV ** -0.5, 3.0)
    conv_bias = scatter_about(splits[3], (XBCW,), 0.5, 3.0, (), jnp.float32)
    a_log = jnp.clip(jax.random.uniform(splits[4], (HEADS,), jnp.float32, -0.2, 0.2), -0.2, 0.2)
    dt_bias = draw_dt_bias(jax.random.fold_in(splits[7], 71), 0)
    d_skip = jnp.clip(1.0 + 0.1 * jax.random.normal(splits[6], (HEADS,), jnp.float32), 0.5, 1.5)
    return {"conv_input": conv_input, "dt_raw": dt_raw, "conv_weight": conv_weight, "conv_bias": conv_bias, "a_log": a_log, "dt_bias": dt_bias, "d_skip": d_skip}


def reference(conv_input, dt_raw, conv_weight, conv_bias, a_log, dt_bias, d_skip):
    f32 = jnp.float32
    x_width = HEADS * HEADDIM
    per_group = HEADS // GROUPS
    width = conv_input.shape[1]
    padded = jnp.concatenate([jnp.zeros((CONV - 1, width), conv_input.dtype), conv_input], 0)
    taps = conv_weight.astype(f32)
    rate = -jnp.exp(a_log)
    tri = lax.broadcasted_iota(jnp.int32, (SPAN, SPAN), 0) >= lax.broadcasted_iota(jnp.int32, (SPAN, SPAN), 1)
    blocks = INPUT_LENGTH // SPAN

    def one_block(state, index):
        start = (index * SPAN).astype(jnp.int32)
        window = lax.dynamic_slice_in_dim(padded, start, SPAN + CONV - 1, 0).astype(f32)
        total = window[0:SPAN] * taps[0]
        for k in range(1, CONV):
            total = total + window[k:k + SPAN] * taps[k]
        act = jax.nn.silu(total + conv_bias).astype(jnp.bfloat16)
        x_act = act[:, :x_width]
        b_act = act[:, x_width:x_width + GROUPS * STATE].reshape(SPAN, GROUPS, STATE).astype(f32)
        c_act = act[:, x_width + GROUPS * STATE:].reshape(SPAN, GROUPS, STATE).astype(f32)
        raw = lax.dynamic_slice_in_dim(dt_raw, start, SPAN, 0).astype(f32)
        step = jax.nn.softplus(raw + dt_bias)
        cum = jnp.cumsum(rate * step, axis=0)
        grams = jnp.einsum('tgn,sgn->gts', c_act, b_act)
        grams = jnp.repeat(grams, per_group, axis=0)
        cum_t = cum.T
        decay = jnp.exp(jnp.where(tri[None], cum_t[:, :, None] - cum_t[:, None, :], -jnp.inf))
        mix = (grams * decay * step.T[:, None, :]).astype(jnp.bfloat16)
        x_heads = x_act.reshape(SPAN, HEADS, HEADDIM).astype(f32)
        y_block = jnp.einsum('hts,shp->thp', mix.astype(f32), x_heads).reshape(SPAN, x_width)
        grown = jnp.repeat(jnp.exp(cum), HEADDIM, axis=1)
        y_state = grown * jnp.einsum('tgn,ngc->tgc', c_act, state.reshape(STATE, GROUPS, per_group * HEADDIM), precision=lax.Precision.HIGHEST).reshape(SPAN, x_width)
        weight = jnp.exp(cum[-1][None, :] - cum) * step
        xw = (x_heads * weight[:, :, None]).astype(jnp.bfloat16).astype(f32)
        contrib = jnp.einsum('sgn,sgc->ngc', b_act, xw.reshape(SPAN, GROUPS, per_group * HEADDIM)).reshape(STATE, x_width)
        fade = jnp.exp(jnp.repeat(cum[-1], HEADDIM))
        new_state = state * fade[None, :] + contrib
        skip = jnp.repeat(d_skip, HEADDIM)
        out = (y_block + y_state + skip * x_act.astype(f32)).astype(jnp.bfloat16)
        return new_state, out

    start_state = jnp.zeros((STATE, x_width), f32)
    final, outs = lax.scan(one_block, start_state, jnp.arange(blocks, dtype=jnp.int32))
    return outs.reshape(INPUT_LENGTH, x_width)
```

```python
import functools

import jax
import jax.numpy as jnp
from jax import lax
from jax.experimental import pallas as pl
from jax.experimental.pallas import tpu as pltpu
from jax.sharding import PartitionSpec as P

HEADS = 256
HEADDIM = 64
STATE = 256
GROUPS = 8
CONV = 4
CHUNK = 128
UNIT = 256
RIM = 16
AHEAD = 3
SKIP_ROW = 126
TOTAL_ROW = 127

F32 = jnp.float32
BF16 = jnp.bfloat16
MESH = pl.DeviceIdType.MESH


def softplus(value):
    z = jnp.exp(-jnp.abs(value))
    s = z / (2.0 + z)
    q = s * s
    series = jnp.full_like(s, 1.0 / 15.0)
    for odd in (13, 11, 9, 7, 5, 3, 1):
        series = series * q + 1.0 / odd
    return jnp.maximum(value, 0.0) + 2.0 * s * series


def dot(a, b, precision=None):
    return jnp.dot(a, b, preferred_element_type=F32, precision=precision)


def kernel(
    n_ctx, n_head,
    x_hbm, dt_ref, w_ref, b_ref, head_ref,
    out_hbm,
    buf, dts, dtr, dtf, daf, b_t, c_act, gram, feat, fade_t, fade, e_u, e_v, e_g, y_buf, state, s_out, s_in,
    send_sem, recv_sem, dt_send, dt_recv, rim_send, rim_recv, chain_send, chain_recv, out_sem,
):
    tok = x_hbm.shape[0]
    length = tok * n_head
    slab = HEADS * HEADDIM // n_head
    hd = HEADS // n_head
    pieces = slab // UNIT
    per_unit = UNIT // HEADDIM
    x_width = HEADS * HEADDIM
    repeat_count = n_head // GROUPS
    n_chunk = length // CHUNK
    ctx = lax.axis_index("ctx")
    me = lax.axis_index("head")
    last = n_head - 1
    turns = sorted(range(1, n_head), key=lambda d: abs(2 * d - n_head))

    def device(c, j):
        return (c, j)

    barrier = pltpu.get_barrier_semaphore()

    def greet(c, j):
        pl.semaphore_signal(barrier, inc=1, device_id=device(c, j), device_id_type=MESH)

    for d in turns:
        greet(ctx, lax.rem(me + d, n_head))

    @pl.when(ctx < n_ctx - 1)
    def _():
        greet(ctx + 1, me)

        @pl.when(me == last)
        def _():
            for j in range(last):
                greet(ctx + 1, j)

    @pl.when(ctx > 0)
    def _():
        greet(ctx - 1, me)

        @pl.when(me < last)
        def _():
            greet(ctx - 1, last)

    def column(q, j):
        if isinstance(q, int) and q < 2:
            return pl.multiple_of(x_width + (q * GROUPS + j // repeat_count) * STATE, UNIT)
        return pl.multiple_of(j * slab + (q - 2) * UNIT, UNIT)

    def place(q):
        return pl.ds(pl.multiple_of(q * UNIT, UNIT), UNIT)

    def landing(q, src):
        return buf.at[pl.ds(pl.multiple_of(RIM + src * tok, RIM), tok), place(q)]

    def unit_copy(q, j):
        return pltpu.make_async_remote_copy(
            src_ref=x_hbm.at[:, pl.ds(column(q, j), UNIT)],
            dst_ref=landing(q, me),
            send_sem=send_sem.at[q, j],
            recv_sem=recv_sem.at[q, me],
            device_id=device(ctx, j),
            device_id_type=MESH,
        )

    def own_copy(q):
        return pltpu.make_async_copy(
            x_hbm.at[:, pl.ds(column(q, me), UNIT)], landing(q, me), recv_sem.at[q, me]
        )

    def unit_start(q):
        for d in turns:
            unit_copy(q, lax.rem(me + d, n_head)).start()
        own_copy(q).start()

    def unit_sent(q):
        for d in turns:
            unit_copy(q, lax.rem(me + d, n_head)).wait_send()

    def unit_arrived(q, src):
        pltpu.make_async_copy(landing(q, src), landing(q, src), recv_sem.at[q, src]).wait()

    def dt_copy(j):
        return pltpu.make_async_remote_copy(
            src_ref=dts.at[pl.ds(pl.multiple_of(j * hd, hd), hd), :],
            dst_ref=dtr.at[:, pl.ds(pl.multiple_of(me * tok, tok), tok)],
            send_sem=dt_send.at[j],
            recv_sem=dt_recv.at[me],
            device_id=device(ctx, j),
            device_id_type=MESH,
        )

    def rim_copy(part, j):
        start = column(part, j) if part < 2 else pl.multiple_of(j * slab, UNIT)
        size = UNIT if part < 2 else slab
        return pltpu.make_async_remote_copy(
            src_ref=x_hbm.at[pl.ds(tok - RIM, RIM), pl.ds(start, size)],
            dst_ref=buf.at[pl.ds(0, RIM), pl.ds(part * UNIT, size)],
            send_sem=rim_send.at[part, j],
            recv_sem=rim_recv.at[part],
            device_id=device(ctx + 1, j),
            device_id_type=MESH,
        )

    def rim_arrived(part):
        size = UNIT if part < 2 else slab
        where = buf.at[pl.ds(0, RIM), pl.ds(part * UNIT, size)]
        pltpu.make_async_copy(where, where, rim_recv.at[part]).wait()

    def chain_copy(p):
        return pltpu.make_async_remote_copy(
            src_ref=s_out.at[p],
            dst_ref=s_in.at[p],
            send_sem=chain_send.at[p],
            recv_sem=chain_recv.at[p],
            device_id=device(ctx + 1, me),
            device_id_type=MESH,
        )

    def out_copy(p):
        return pltpu.make_async_copy(
            buf.at[pl.ds(RIM, length), place(p + 2)], out_hbm.at[:, place(p)], out_sem.at[p]
        )

    dts[...] = dt_ref[...].astype(F32).T.astype(BF16)

    @pl.when(ctx == 0)
    def _():
        buf[0:RIM, :] = jnp.zeros((RIM, buf.shape[1]), BF16)
        s_in[...] = jnp.zeros(s_in.shape, F32)

    has_next = (ctx < n_ctx - 1).astype(jnp.int32)
    has_prev = (ctx > 0).astype(jnp.int32)
    is_last = (me == last).astype(jnp.int32)
    pl.semaphore_wait(
        barrier, last + has_next * (1 + last * is_last) + has_prev * (2 - is_last)
    )

    for d in turns:
        dt_copy(lax.rem(me + d, n_head)).start()
    own_dt = pltpu.make_async_copy(
        dts.at[pl.ds(pl.multiple_of(me * hd, hd), hd), :],
        dtr.at[:, pl.ds(pl.multiple_of(me * tok, tok), tok)],
        dt_recv.at[me],
    )
    own_dt.start()

    sends_rim = jnp.logical_and(ctx < n_ctx - 1, me == last)

    @pl.when(sends_rim)
    def _():
        for part in range(3):
            for j in range(n_head):
                rim_copy(part, j).start()

    unit_start(0)
    unit_start(1)
    for p in range(min(AHEAD, pieces)):
        unit_start(p + 2)

    for src in range(n_head):
        where = dtr.at[:, pl.ds(src * tok, tok)]
        pltpu.make_async_copy(where, where, dt_recv.at[src]).wait()
    mine = pl.ds(pl.multiple_of(me * hd, hd), hd)
    per_head = head_ref[mine, :]
    dt_now = softplus(dtr[...].astype(F32) + per_head[:, 1:2])
    dtf[...] = dt_now
    daf[...] = -jnp.exp(per_head[:, 0:1]) * dt_now
    upto = (
        lax.broadcasted_iota(jnp.int32, (CHUNK, CHUNK), 0)
        <= lax.broadcasted_iota(jnp.int32, (CHUNK, CHUNK), 1)
    ).astype(F32)
    lane = lax.broadcasted_iota(jnp.int32, (hd, 128), 1)

    def factors(k, carry):
        start, expo = carry
        span = pl.ds(pl.multiple_of(k * CHUNK, CHUNK), CHUNK)
        cum = dot(daf[:, span], upto, lax.Precision.HIGHEST)
        mid = cum[:, CHUNK // 2 - 1 : CHUNK // 2]
        end = cum[:, CHUNK - 1 : CHUNK]
        parts = []
        for value in (jnp.exp(cum - mid), jnp.exp(mid - cum) * dtf[:, span], jnp.exp(start + cum)):
            high = value.astype(BF16).astype(F32)
            parts += [high, value - high]
        zero = jnp.zeros((hd, CHUNK), F32)
        feat[span, :] = jnp.concatenate(parts + [zero, zero], 0).T.astype(BF16)
        expo = expo + jnp.where(lane == k, end - mid, 0.0)
        expo = expo + jnp.where(lane == k - 1, mid, 0.0)
        expo = expo + jnp.where(lane == TOTAL_ROW, end, 0.0)
        return start + end, expo

    _, expo = lax.fori_loop(
        0, n_chunk, factors, (jnp.zeros((hd, 1), F32), jnp.zeros((hd, 128), F32))
    )
    fade_t[...] = jnp.where(lane == SKIP_ROW, per_head[:, 2:3], jnp.exp(expo)).T

    def conv(q, start, src):
        cols = pl.ds(start, UNIT)
        taps = w_ref[:, cols].astype(F32)
        window = buf[pl.ds(pl.multiple_of(src * tok, RIM), tok + RIM), place(q)].astype(F32)
        first = RIM - (CONV - 1)
        total = window[first : first + tok] * taps[0:1]
        for k in range(1, CONV):
            total = total + window[first + k : first + k + tok] * taps[k : k + 1]
        total = total + b_ref[:, cols]
        return (total / (1.0 + jnp.exp(-total))).astype(BF16)

    @pl.when(ctx > 0)
    def _():
        for part in range(3):
            rim_arrived(part)

    causal = lax.broadcasted_iota(jnp.int32, (CHUNK, CHUNK), 0) >= lax.broadcasted_iota(
        jnp.int32, (CHUNK, CHUNK), 1
    )

    def projections(src, _):
        unit_arrived(0, src)
        unit_arrived(1, src)
        b_now = conv(0, column(0, me), src)
        c_now = conv(1, column(1, me), src)
        rows = pl.ds(pl.multiple_of(src * tok, tok), tok)
        b_t[:, rows] = b_now.astype(F32).T.astype(BF16)
        c_act[rows, :] = c_now
        for i in range(tok // CHUNK):
            part = slice(i * CHUNK, (i + 1) * CHUNK)
            inner = lax.dot_general(
                c_now[part], b_now[part], (((1,), (1,)), ((), ())), preferred_element_type=F32
            )
            gram[pl.ds(pl.multiple_of(src * tok + i * CHUNK, CHUNK), CHUNK), :] = jnp.where(
                causal, inner, 0.0
            ).astype(BF16)
        return 0

    lax.fori_loop(0, n_head, projections, 0)
    unit_sent(0)
    unit_sent(1)

    row = lax.broadcasted_iota(jnp.int32, (8 * hd, UNIT), 0)
    col = lax.broadcasted_iota(jnp.int32, (8 * hd, UNIT), 1) // HEADDIM

    def spread(p, at):
        head = col + p * per_unit
        hit = jnp.logical_or(row == head + at * hd, row == head + (at + 1) * hd)
        return jnp.where(hit, 1.0, 0.0).astype(BF16)

    def finish(p):
        @pl.when(ctx > 0)
        def _():
            pltpu.make_async_copy(s_in.at[p], s_in.at[p], chain_recv.at[p]).wait()

        slot = lax.rem(p, 2)

        @pl.when(jnp.logical_and(ctx > 0, ctx < n_ctx - 1))
        def _():
            s_out[p] = fade[slot, TOTAL_ROW : TOTAL_ROW + 1, :] * s_in[p] + s_out[p]
            chain_copy(p).start()

        e_g[...] = spread(p, 4)

        def block(i, _):
            rows = pl.ds(pl.multiple_of(i * tok, tok), tok)
            grown = dot(feat[rows, :], e_g[...])
            late = grown * dot(c_act[rows, :], s_in[p].astype(BF16))
            buf[pl.ds(pl.multiple_of(RIM + i * tok, RIM), tok), place(p + 2)] = (
                y_buf[slot, rows, :] + late
            ).astype(BF16)
            return 0

        lax.fori_loop(0, n_head, block, 0)
        out_copy(p).start()

    def piece(p, _):
        unit_sent(p + 2)

        @pl.when(p + AHEAD < pieces)
        def _():
            unit_start(p + AHEAD + 2)

        slot = lax.rem(p, 2)
        e_u[...] = spread(p, 0)
        e_v[...] = spread(p, 2)
        expand = jnp.where(row[0:hd] == col[0:hd] + p * per_unit, 1.0, 0.0)
        fade[slot] = dot(fade_t[...], expand, lax.Precision.HIGHEST)
        state[...] = jnp.zeros(state.shape, F32)

        def block(src, _):
            unit_arrived(p + 2, src)
            act = conv(p + 2, column(p + 2, me), src).astype(F32)
            rows = pl.ds(pl.multiple_of(src * tok, tok), tok)
            grow = dot(feat[rows, :], e_u[...])
            scaled = (act * dot(feat[rows, :], e_v[...])).astype(BF16)
            for i in range(tok // CHUNK):
                part = slice(i * CHUNK, (i + 1) * CHUNK)
                span = pl.ds(pl.multiple_of(src * tok + i * CHUNK, CHUNK), CHUNK)
                entering = state[...]
                y = dot(gram[span, :], scaled[part]) + dot(c_act[span, :], entering.astype(BF16))
                y_buf[slot, span, :] = (
                    grow[part] * y + fade[slot, SKIP_ROW : SKIP_ROW + 1, :] * act[part]
                )
                added = dot(b_t[:, span], scaled[part])
                k = src * (tok // CHUNK) + i
                state[...] = fade[slot, pl.ds(k, 1), :] * (entering + added)
            return 0

        lax.fori_loop(0, n_head, block, 0)
        s_out[p] = state[...]

        @pl.when(ctx == 0)
        def _():
            chain_copy(p).start()

        @pl.when(p > 0)
        def _():
            finish(p - 1)

        return 0

    lax.fori_loop(0, pieces, piece, 0)
    finish(pieces - 1)

    for d in turns:
        dt_copy(lax.rem(me + d, n_head)).wait_send()

    @pl.when(sends_rim)
    def _():
        for part in range(3):
            for j in range(n_head):
                rim_copy(part, j).wait_send()

    @pl.when(ctx < n_ctx - 1)
    def _():
        for p in range(pieces):
            chain_copy(p).wait_send()

    for p in range(pieces):
        out_copy(p).wait()


def on_device(conv_input, dt_raw, conv_weight, conv_bias, a_log, dt_bias, d_skip):
    n_ctx, n_head = lax.axis_size("ctx"), lax.axis_size("head")
    tok = conv_input.shape[0]
    length = tok * n_head
    slab = HEADS * HEADDIM // n_head
    hd = HEADS // n_head
    pieces = slab // UNIT
    per_head = jnp.stack([a_log, dt_bias, d_skip], 1)
    vmem = pl.BlockSpec(memory_space=pltpu.VMEM)
    anywhere = pl.BlockSpec(memory_space=pl.ANY)
    dma = pltpu.SemaphoreType.DMA
    return pl.pallas_call(
        functools.partial(kernel, n_ctx, n_head),
        out_shape=jax.ShapeDtypeStruct((length, slab), BF16),
        in_specs=[anywhere, vmem, vmem, vmem, vmem],
        out_specs=anywhere,
        scratch_shapes=[
            pltpu.VMEM((RIM + length, slab + 2 * STATE), BF16),
            pltpu.VMEM((HEADS, tok), BF16),
            pltpu.VMEM((hd, length), BF16),
            pltpu.VMEM((hd, length), F32),
            pltpu.VMEM((hd, length), F32),
            pltpu.VMEM((STATE, length), BF16),
            pltpu.VMEM((length, STATE), BF16),
            pltpu.VMEM((length, CHUNK), BF16),
            pltpu.VMEM((length, 8 * hd), BF16),
            pltpu.VMEM((128, hd), F32),
            pltpu.VMEM((2, 128, UNIT), F32),
            pltpu.VMEM((8 * hd, UNIT), BF16),
            pltpu.VMEM((8 * hd, UNIT), BF16),
            pltpu.VMEM((8 * hd, UNIT), BF16),
            pltpu.VMEM((2, length, UNIT), F32),
            pltpu.VMEM((STATE, UNIT), F32),
            pltpu.VMEM((pieces, STATE, UNIT), F32),
            pltpu.VMEM((pieces, STATE, UNIT), F32),
            dma((pieces + 2, n_head)),
            dma((pieces + 2, n_head)),
            dma((n_head,)),
            dma((n_head,)),
            dma((3, n_head)),
            dma((3,)),
            dma((pieces,)),
            dma((pieces,)),
            dma((pieces,)),
        ],
        compiler_params=pltpu.CompilerParams(
            collective_id=0, has_side_effects=True, vmem_limit_bytes=56 * 1024 * 1024
        ),
    )(conv_input, dt_raw, conv_weight, conv_bias.reshape(1, -1), per_head)


def solution(mesh):
    placed = (P(("ctx", "head"), None), P(("ctx", "head"), None), P(), P(), P(), P(), P())
    return jax.shard_map(
        on_device, mesh=mesh, in_specs=placed, out_specs=P("ctx", "head"), check_vma=False
    )
```

```python
import functools

import jax
import jax.numpy as jnp
from jax import lax
from jax.experimental import pallas as pl
from jax.experimental.pallas import tpu as pltpu
from jax.sharding import PartitionSpec as P

HEADS = 256
HEADDIM = 64
STATE = 256
GROUPS = 8
CONV = 4
CHUNK = 128
UNIT = 256
RIM = 16
AHEAD = 2
SKIP_ROW = 126
TOTAL_ROW = 127

F32 = jnp.float32
BF16 = jnp.bfloat16
MESH = pl.DeviceIdType.MESH


def softplus(value):
    z = jnp.exp(-jnp.abs(value))
    s = z / (2.0 + z)
    q = s * s
    series = jnp.full_like(s, 1.0 / 15.0)
    for odd in (13, 11, 9, 7, 5, 3, 1):
        series = series * q + 1.0 / odd
    return jnp.maximum(value, 0.0) + 2.0 * s * series


def dot(a, b, precision=None):
    return jnp.dot(a, b, preferred_element_type=F32, precision=precision)


def kernel(
    n_ctx, n_head,
    x_hbm, dt_ref, w_ref, b_ref, a_ref, bias_ref, skip_ref,
    out_hbm,
    buf, heads, dts, dtr, dtf, daf, b_t, c_act, gram, feat, fade_t, fade, e_u, e_v, e_g, y_buf, state, s_out, s_in,
    send_sem, recv_sem, dt_send, dt_recv, rim_send, rim_recv, chain_send, chain_recv, out_sem,
):
    tok = x_hbm.shape[0]
    length = tok * n_head
    slab = HEADS * HEADDIM // n_head
    hd = HEADS // n_head
    pieces = slab // UNIT
    per_unit = UNIT // HEADDIM
    x_width = HEADS * HEADDIM
    repeat_count = n_head // GROUPS
    n_chunk = length // CHUNK
    ctx = lax.axis_index("ctx")
    me = lax.axis_index("head")
    last = n_head - 1
    turns = sorted(range(1, n_head), key=lambda d: abs(2 * d - n_head))

    def device(c, j):
        return (c, j)

    barrier = pltpu.get_barrier_semaphore()

    def greet(c, j):
        pl.semaphore_signal(barrier, inc=1, device_id=device(c, j), device_id_type=MESH)

    for d in turns:
        greet(ctx, lax.rem(me + d, n_head))

    @pl.when(ctx < n_ctx - 1)
    def _():
        greet(ctx + 1, me)

        @pl.when(me == last)
        def _():
            for j in range(last):
                greet(ctx + 1, j)

    @pl.when(ctx > 0)
    def _():
        greet(ctx - 1, me)

        @pl.when(me < last)
        def _():
            greet(ctx - 1, last)

    def column(q, j):
        if isinstance(q, int) and q < 2:
            return pl.multiple_of(x_width + (q * GROUPS + j // repeat_count) * STATE, UNIT)
        return pl.multiple_of(j * slab + (q - 2) * UNIT, UNIT)

    def place(q):
        return pl.ds(pl.multiple_of(q * UNIT, UNIT), UNIT)

    def landing(q, src):
        return buf.at[pl.ds(pl.multiple_of(RIM + src * tok, RIM), tok), place(q)]

    def unit_copy(q, j):
        return pltpu.make_async_remote_copy(
            src_ref=x_hbm.at[:, pl.ds(column(q, j), UNIT)],
            dst_ref=landing(q, me),
            send_sem=send_sem.at[q, j],
            recv_sem=recv_sem.at[q, me],
            device_id=device(ctx, j),
            device_id_type=MESH,
        )

    def own_copy(q):
        return pltpu.make_async_copy(
            x_hbm.at[:, pl.ds(column(q, me), UNIT)], landing(q, me), recv_sem.at[q, me]
        )

    def unit_start(q):
        for d in turns:
            unit_copy(q, lax.rem(me + d, n_head)).start()
        own_copy(q).start()

    def unit_sent(q):
        for d in turns:
            unit_copy(q, lax.rem(me + d, n_head)).wait_send()

    def unit_arrived(q, src):
        pltpu.make_async_copy(landing(q, src), landing(q, src), recv_sem.at[q, src]).wait()

    def dt_copy(j):
        return pltpu.make_async_remote_copy(
            src_ref=dts.at[pl.ds(pl.multiple_of(j * hd, hd), hd), :],
            dst_ref=dtr.at[:, pl.ds(pl.multiple_of(me * tok, tok), tok)],
            send_sem=dt_send.at[j],
            recv_sem=dt_recv.at[me],
            device_id=device(ctx, j),
            device_id_type=MESH,
        )

    def rim_copy(part, j):
        start = column(part, j) if part < 2 else pl.multiple_of(j * slab, UNIT)
        size = UNIT if part < 2 else slab
        return pltpu.make_async_remote_copy(
            src_ref=x_hbm.at[pl.ds(tok - RIM, RIM), pl.ds(start, size)],
            dst_ref=buf.at[pl.ds(0, RIM), pl.ds(part * UNIT, size)],
            send_sem=rim_send.at[part, j],
            recv_sem=rim_recv.at[part],
            device_id=device(ctx + 1, j),
            device_id_type=MESH,
        )

    def rim_arrived(part):
        size = UNIT if part < 2 else slab
        where = buf.at[pl.ds(0, RIM), pl.ds(part * UNIT, size)]
        pltpu.make_async_copy(where, where, rim_recv.at[part]).wait()

    def chain_copy(p):
        return pltpu.make_async_remote_copy(
            src_ref=s_out.at[p],
            dst_ref=s_in.at[p],
            send_sem=chain_send.at[p],
            recv_sem=chain_recv.at[p],
            device_id=device(ctx + 1, me),
            device_id_type=MESH,
        )

    def out_copy(p):
        return pltpu.make_async_copy(
            buf.at[pl.ds(RIM, length), place(p + 2)], out_hbm.at[:, place(p)], out_sem.at[p]
        )

    has_next = (ctx < n_ctx - 1).astype(jnp.int32)
    has_prev = (ctx > 0).astype(jnp.int32)
    is_last = (me == last).astype(jnp.int32)
    pl.semaphore_wait(
        barrier, last + has_next * (1 + last * is_last) + has_prev * (2 - is_last)
    )

    unit_start(0)
    unit_start(1)
    dts[...] = dt_ref[...].astype(F32).T.astype(BF16)
    for d in turns:
        dt_copy(lax.rem(me + d, n_head)).start()
    own_dt = pltpu.make_async_copy(
        dts.at[pl.ds(pl.multiple_of(me * hd, hd), hd), :],
        dtr.at[:, pl.ds(pl.multiple_of(me * tok, tok), tok)],
        dt_recv.at[me],
    )
    own_dt.start()

    sends_rim = jnp.logical_and(ctx < n_ctx - 1, me == last)

    @pl.when(sends_rim)
    def _():
        for part in range(3):
            for j in range(n_head):
                rim_copy(part, j).start()

    for p in range(min(AHEAD, pieces)):
        unit_start(p + 2)

    @pl.when(ctx == 0)
    def _():
        buf[0:RIM, :] = jnp.zeros((RIM, buf.shape[1]), BF16)
        s_in[...] = jnp.zeros(s_in.shape, BF16)

    heads[...] = jnp.concatenate(
        [a_ref[...], bias_ref[...], skip_ref[...], jnp.zeros((5, HEADS), F32)], 0
    ).T

    for src in range(n_head):
        where = dtr.at[:, pl.ds(src * tok, tok)]
        pltpu.make_async_copy(where, where, dt_recv.at[src]).wait()
    mine = pl.ds(pl.multiple_of(me * hd, hd), hd)
    per_head = heads[mine, :]
    dt_now = softplus(dtr[...].astype(F32) + per_head[:, 1:2])
    dtf[...] = dt_now
    daf[...] = -jnp.exp(per_head[:, 0:1]) * dt_now
    upto = (
        lax.broadcasted_iota(jnp.int32, (CHUNK, CHUNK), 0)
        <= lax.broadcasted_iota(jnp.int32, (CHUNK, CHUNK), 1)
    ).astype(F32)
    lane = lax.broadcasted_iota(jnp.int32, (hd, 128), 1)

    def factors(k, carry):
        start, expo = carry
        span = pl.ds(pl.multiple_of(k * CHUNK, CHUNK), CHUNK)
        cum = dot(daf[:, span], upto, lax.Precision.HIGHEST)
        mid = cum[:, CHUNK // 2 - 1 : CHUNK // 2]
        end = cum[:, CHUNK - 1 : CHUNK]
        parts = []
        for value in (jnp.exp(cum - mid), jnp.exp(mid - cum) * dtf[:, span], jnp.exp(start + cum)):
            high = value.astype(BF16).astype(F32)
            parts += [high, value - high]
        zero = jnp.zeros((hd, CHUNK), F32)
        feat[span, :] = jnp.concatenate(parts + [zero, zero], 0).T.astype(BF16)
        expo = expo + jnp.where(lane == k, end - mid, 0.0)
        expo = expo + jnp.where(lane == k - 1, mid, 0.0)
        expo = expo + jnp.where(lane == TOTAL_ROW, end, 0.0)
        return start + end, expo

    _, expo = lax.fori_loop(
        0, n_chunk, factors, (jnp.zeros((hd, 1), F32), jnp.zeros((hd, 128), F32))
    )
    fade_t[...] = jnp.where(lane == SKIP_ROW, per_head[:, 2:3], jnp.exp(expo)).T

    def conv(q, start, src):
        cols = pl.ds(start, UNIT)
        taps = w_ref[:, cols].astype(F32)
        window = buf[pl.ds(pl.multiple_of(src * tok, RIM), tok + RIM), place(q)].astype(F32)
        first = RIM - (CONV - 1)
        total = window[first : first + tok] * taps[0:1]
        for k in range(1, CONV):
            total = total + window[first + k : first + k + tok] * taps[k : k + 1]
        total = total + b_ref[:, cols]
        return (total / (1.0 + jnp.exp(-total))).astype(BF16)

    @pl.when(ctx > 0)
    def _():
        for part in range(3):
            rim_arrived(part)

    causal = lax.broadcasted_iota(jnp.int32, (CHUNK, CHUNK), 0) >= lax.broadcasted_iota(
        jnp.int32, (CHUNK, CHUNK), 1
    )

    def projections(src, _):
        unit_arrived(0, src)
        unit_arrived(1, src)
        b_now = conv(0, column(0, me), src)
        c_now = conv(1, column(1, me), src)
        rows = pl.ds(pl.multiple_of(src * tok, tok), tok)
        b_t[:, rows] = b_now.astype(F32).T.astype(BF16)
        c_act[rows, :] = c_now
        for i in range(tok // CHUNK):
            part = slice(i * CHUNK, (i + 1) * CHUNK)
            inner = lax.dot_general(
                c_now[part], b_now[part], (((1,), (1,)), ((), ())), preferred_element_type=F32
            )
            gram[pl.ds(pl.multiple_of(src * tok + i * CHUNK, CHUNK), CHUNK), :] = jnp.where(
                causal, inner, 0.0
            ).astype(BF16)
        return 0

    lax.fori_loop(0, n_head, projections, 0)
    unit_sent(0)
    unit_sent(1)

    row = lax.broadcasted_iota(jnp.int32, (8 * hd, UNIT), 0)
    col = lax.broadcasted_iota(jnp.int32, (8 * hd, UNIT), 1) // HEADDIM

    def spread(p, at):
        head = col + p * per_unit
        hit = jnp.logical_or(row == head + at * hd, row == head + (at + 1) * hd)
        return jnp.where(hit, 1.0, 0.0).astype(BF16)

    def finish(p):
        @pl.when(ctx > 0)
        def _():
            pltpu.make_async_copy(s_in.at[p], s_in.at[p], chain_recv.at[p]).wait()

        @pl.when(ctx < n_ctx - 1)
        def _():
            before = s_in[p].astype(F32)
            s_out[p] = (fade[TOTAL_ROW : TOTAL_ROW + 1, :] * before + state[...]).astype(BF16)
            chain_copy(p).start()

        e_g[...] = spread(p, 4)

        def block(i, _):
            rows = pl.ds(pl.multiple_of(i * tok, tok), tok)
            grown = dot(feat[rows, :], e_g[...])
            late = grown * dot(c_act[rows, :], s_in[p])
            buf[pl.ds(pl.multiple_of(RIM + i * tok, RIM), tok), place(p + 2)] = (
                y_buf[rows, :] + late
            ).astype(BF16)
            return 0

        lax.fori_loop(0, n_head, block, 0)
        out_copy(p).start()

    def piece(p, _):
        unit_sent(p + 2)

        @pl.when(p + AHEAD < pieces)
        def _():
            unit_start(p + AHEAD + 2)

        e_u[...] = spread(p, 0)
        e_v[...] = spread(p, 2)
        expand = jnp.where(row[0:hd] == col[0:hd] + p * per_unit, 1.0, 0.0)
        fade[...] = dot(fade_t[...], expand, lax.Precision.HIGHEST)
        state[...] = jnp.zeros(state.shape, F32)

        def block(src, _):
            unit_arrived(p + 2, src)
            act = conv(p + 2, column(p + 2, me), src).astype(F32)
            rows = pl.ds(pl.multiple_of(src * tok, tok), tok)
            grow = dot(feat[rows, :], e_u[...])
            scaled = (act * dot(feat[rows, :], e_v[...])).astype(BF16)
            for i in range(tok // CHUNK):
                part = slice(i * CHUNK, (i + 1) * CHUNK)
                span = pl.ds(pl.multiple_of(src * tok + i * CHUNK, CHUNK), CHUNK)
                entering = state[...]
                y = dot(gram[span, :], scaled[part]) + dot(c_act[span, :], entering.astype(BF16))
                y_buf[span, :] = (
                    grow[part] * y + fade[SKIP_ROW : SKIP_ROW + 1, :] * act[part]
                )
                added = dot(b_t[:, span], scaled[part])
                k = src * (tok // CHUNK) + i
                state[...] = fade[pl.ds(k, 1), :] * (entering + added)
            return 0

        lax.fori_loop(0, n_head, block, 0)
        finish(p)
        return 0

    lax.fori_loop(0, pieces, piece, 0)

    for d in turns:
        dt_copy(lax.rem(me + d, n_head)).wait_send()

    @pl.when(sends_rim)
    def _():
        for part in range(3):
            for j in range(n_head):
                rim_copy(part, j).wait_send()

    @pl.when(ctx < n_ctx - 1)
    def _():
        for p in range(pieces):
            chain_copy(p).wait_send()

    for p in range(pieces):
        out_copy(p).wait()


def on_device(conv_input, dt_raw, conv_weight, conv_bias, a_log, dt_bias, d_skip):
    n_ctx, n_head = lax.axis_size("ctx"), lax.axis_size("head")
    tok = conv_input.shape[0]
    length = tok * n_head
    slab = HEADS * HEADDIM // n_head
    hd = HEADS // n_head
    pieces = slab // UNIT
    vmem = pl.BlockSpec(memory_space=pltpu.VMEM)
    anywhere = pl.BlockSpec(memory_space=pl.ANY)
    dma = pltpu.SemaphoreType.DMA
    return pl.pallas_call(
        functools.partial(kernel, n_ctx, n_head),
        out_shape=jax.ShapeDtypeStruct((length, slab), BF16),
        in_specs=[anywhere] + [vmem] * 6,
        out_specs=anywhere,
        scratch_shapes=[
            pltpu.VMEM((RIM + length, slab + 2 * STATE), BF16),
            pltpu.VMEM((HEADS, 8), F32),
            pltpu.VMEM((HEADS, tok), BF16),
            pltpu.VMEM((hd, length), BF16),
            pltpu.VMEM((hd, length), F32),
            pltpu.VMEM((hd, length), F32),
            pltpu.VMEM((STATE, length), BF16),
            pltpu.VMEM((length, STATE), BF16),
            pltpu.VMEM((length, CHUNK), BF16),
            pltpu.VMEM((length, 8 * hd), BF16),
            pltpu.VMEM((128, hd), F32),
            pltpu.VMEM((128, UNIT), F32),
            pltpu.VMEM((8 * hd, UNIT), BF16),
            pltpu.VMEM((8 * hd, UNIT), BF16),
            pltpu.VMEM((8 * hd, UNIT), BF16),
            pltpu.VMEM((length, UNIT), F32),
            pltpu.VMEM((STATE, UNIT), F32),
            pltpu.VMEM((pieces, STATE, UNIT), BF16),
            pltpu.VMEM((pieces, STATE, UNIT), BF16),
            dma((pieces + 2, n_head)),
            dma((pieces + 2, n_head)),
            dma((n_head,)),
            dma((n_head,)),
            dma((3, n_head)),
            dma((3,)),
            dma((pieces,)),
            dma((pieces,)),
            dma((pieces,)),
        ],
        compiler_params=pltpu.CompilerParams(
            collective_id=0, has_side_effects=True, vmem_limit_bytes=40 * 1024 * 1024
        ),
    )(
        conv_input,
        dt_raw,
        conv_weight,
        *(table.reshape(1, -1) for table in (conv_bias, a_log, dt_bias, d_skip)),
    )


def solution(mesh):
    placed = (P(("ctx", "head"), None), P(("ctx", "head"), None), P(), P(), P(), P(), P())
    return jax.shard_map(
        on_device, mesh=mesh, in_specs=placed, out_specs=P("ctx", "head"), check_vma=False
    )
```

```python
import functools

import jax
import jax.numpy as jnp
from jax import lax
from jax.experimental import pallas as pl
from jax.experimental.pallas import tpu as pltpu
from jax.sharding import PartitionSpec as P

HEADS = 256
HEADDIM = 64
STATE = 256
GROUPS = 8
CONV = 4
CHUNK = 128
UNIT = 256
RIM = 16
AHEAD = 2
PARTS = 16
SKIP_ROW = 126
TOTAL_ROW = 127

F32 = jnp.float32
BF16 = jnp.bfloat16
MESH = pl.DeviceIdType.MESH


def softplus(value):
    z = jnp.exp(-jnp.abs(value))
    s = z / (2.0 + z)
    q = s * s
    series = jnp.full_like(s, 1.0 / 15.0)
    for odd in (13, 11, 9, 7, 5, 3, 1):
        series = series * q + 1.0 / odd
    return jnp.maximum(value, 0.0) + 2.0 * s * series


def dot(a, b, precision=None):
    return jnp.dot(a, b, preferred_element_type=F32, precision=precision)


def kernel(
    n_ctx, n_head,
    x_hbm, dt_hbm, w_hbm, b_hbm, a_hbm, bias_hbm, skip_hbm,
    out_hbm,
    dt_ref, w_ref, b_ref, a_ref, bias_ref, skip_ref, buf, heads, dts, dtr, dtf, daf, b_t, c_act, gram, feat, fade_t, fade, e_u, e_v, e_g, y_buf, state, s_out, s_in,
    send_sem, recv_sem, dt_send, dt_recv, rim_send, rim_recv, chain_send, chain_recv, out_sem, load_sem,
):
    tok = x_hbm.shape[0]
    length = tok * n_head
    slab = HEADS * HEADDIM // n_head
    hd = HEADS // n_head
    pieces = slab // UNIT
    per_unit = UNIT // HEADDIM
    x_width = HEADS * HEADDIM
    repeat_count = n_head // GROUPS
    n_chunk = length // CHUNK
    ctx = lax.axis_index("ctx")
    me = lax.axis_index("head")
    last = n_head - 1
    turns = sorted(range(1, n_head), key=lambda d: abs(2 * d - n_head))

    def device(c, j):
        return (c, j)

    loads = [
        pltpu.make_async_copy(source, held, load_sem.at[i])
        for i, (source, held) in enumerate(
            (
                (dt_hbm, dt_ref),
                (w_hbm, w_ref),
                (b_hbm, b_ref),
                (a_hbm, a_ref),
                (bias_hbm, bias_ref),
                (skip_hbm, skip_ref),
            )
        )
    ]
    for load in loads:
        load.start()

    barrier = pltpu.get_barrier_semaphore()

    def greet(c, j):
        pl.semaphore_signal(barrier, inc=1, device_id=device(c, j), device_id_type=MESH)

    for d in turns:
        greet(ctx, lax.rem(me + d, n_head))

    @pl.when(ctx < n_ctx - 1)
    def _():
        greet(ctx + 1, me)

        @pl.when(me == last)
        def _():
            for j in range(last):
                greet(ctx + 1, j)

    @pl.when(ctx > 0)
    def _():
        greet(ctx - 1, me)

        @pl.when(me < last)
        def _():
            greet(ctx - 1, last)

    def column(q, j):
        if isinstance(q, int) and q < 2:
            return pl.multiple_of(x_width + (q * GROUPS + j // repeat_count) * STATE, UNIT)
        return pl.multiple_of(j * slab + (q - 2) * UNIT, UNIT)

    def place(q):
        return pl.ds(pl.multiple_of(q * UNIT, UNIT), UNIT)

    def landing(q, src):
        return buf.at[pl.ds(pl.multiple_of(RIM + src * tok, RIM), tok), place(q)]

    def unit_copy(q, j):
        return pltpu.make_async_remote_copy(
            src_ref=x_hbm.at[:, pl.ds(column(q, j), UNIT)],
            dst_ref=landing(q, me),
            send_sem=send_sem.at[q, j],
            recv_sem=recv_sem.at[q, me],
            device_id=device(ctx, j),
            device_id_type=MESH,
        )

    def own_copy(q):
        return pltpu.make_async_copy(
            x_hbm.at[:, pl.ds(column(q, me), UNIT)], landing(q, me), recv_sem.at[q, me]
        )

    def unit_start(q):
        for d in turns:
            unit_copy(q, lax.rem(me + d, n_head)).start()
        own_copy(q).start()

    def unit_sent(q):
        for d in turns:
            unit_copy(q, lax.rem(me + d, n_head)).wait_send()

    def unit_arrived(q, src):
        pltpu.make_async_copy(landing(q, src), landing(q, src), recv_sem.at[q, src]).wait()

    def dt_copy(j):
        return pltpu.make_async_remote_copy(
            src_ref=dts.at[pl.ds(pl.multiple_of(j * hd, hd), hd), :],
            dst_ref=dtr.at[:, pl.ds(pl.multiple_of(me * tok, tok), tok)],
            send_sem=dt_send.at[j],
            recv_sem=dt_recv.at[me],
            device_id=device(ctx, j),
            device_id_type=MESH,
        )

    def rim_copy(part, j):
        start = column(part, j) if part < 2 else pl.multiple_of(j * slab, UNIT)
        size = UNIT if part < 2 else slab
        return pltpu.make_async_remote_copy(
            src_ref=x_hbm.at[pl.ds(tok - RIM, RIM), pl.ds(start, size)],
            dst_ref=buf.at[pl.ds(0, RIM), pl.ds(part * UNIT, size)],
            send_sem=rim_send.at[part, j],
            recv_sem=rim_recv.at[part],
            device_id=device(ctx + 1, j),
            device_id_type=MESH,
        )

    def rim_arrived(part):
        size = UNIT if part < 2 else slab
        where = buf.at[pl.ds(0, RIM), pl.ds(part * UNIT, size)]
        pltpu.make_async_copy(where, where, rim_recv.at[part]).wait()

    def chain_copy(p):
        return pltpu.make_async_remote_copy(
            src_ref=s_out.at[p],
            dst_ref=s_in.at[p],
            send_sem=chain_send.at[p],
            recv_sem=chain_recv.at[p],
            device_id=device(ctx + 1, me),
            device_id_type=MESH,
        )

    def out_copy(p):
        return pltpu.make_async_copy(
            buf.at[pl.ds(RIM, length), place(p + 2)], out_hbm.at[:, place(p)], out_sem.at[p]
        )

    has_next = (ctx < n_ctx - 1).astype(jnp.int32)
    has_prev = (ctx > 0).astype(jnp.int32)
    is_last = (me == last).astype(jnp.int32)
    pl.semaphore_wait(
        barrier, last + has_next * (1 + last * is_last) + has_prev * (2 - is_last)
    )

    unit_start(0)
    unit_start(1)
    for load in loads:
        load.wait()
    dts[...] = dt_ref[...].astype(F32).T.astype(BF16)
    for d in turns:
        dt_copy(lax.rem(me + d, n_head)).start()
    own_dt = pltpu.make_async_copy(
        dts.at[pl.ds(pl.multiple_of(me * hd, hd), hd), :],
        dtr.at[:, pl.ds(pl.multiple_of(me * tok, tok), tok)],
        dt_recv.at[me],
    )
    own_dt.start()

    sends_rim = jnp.logical_and(ctx < n_ctx - 1, me == last)

    @pl.when(sends_rim)
    def _():
        for part in range(3):
            for j in range(n_head):
                rim_copy(part, j).start()

    for p in range(min(AHEAD, pieces)):
        unit_start(p + 2)

    @pl.when(ctx == 0)
    def _():
        buf[0:RIM, :] = jnp.zeros((RIM, buf.shape[1]), BF16)
        s_in[...] = jnp.zeros(s_in.shape, BF16)

    heads[...] = jnp.concatenate(
        [a_ref[...], bias_ref[...], skip_ref[...], jnp.zeros((5, HEADS), F32)], 0
    ).T

    for src in range(n_head):
        where = dtr.at[:, pl.ds(src * tok, tok)]
        pltpu.make_async_copy(where, where, dt_recv.at[src]).wait()
    mine = pl.ds(pl.multiple_of(me * hd, hd), hd)
    per_head = heads[mine, :]
    dt_now = softplus(dtr[...].astype(F32) + per_head[:, 1:2])
    dtf[...] = dt_now
    daf[...] = -jnp.exp(per_head[:, 0:1]) * dt_now
    upto = (
        lax.broadcasted_iota(jnp.int32, (CHUNK, CHUNK), 0)
        <= lax.broadcasted_iota(jnp.int32, (CHUNK, CHUNK), 1)
    ).astype(F32)
    lane = lax.broadcasted_iota(jnp.int32, (hd, 128), 1)

    def factors(k, carry):
        start, expo = carry
        span = pl.ds(pl.multiple_of(k * CHUNK, CHUNK), CHUNK)
        cum = dot(daf[:, span], upto, lax.Precision.HIGHEST)
        mid = cum[:, CHUNK // 2 - 1 : CHUNK // 2]
        end = cum[:, CHUNK - 1 : CHUNK]
        parts = []
        for value in (jnp.exp(cum - mid), jnp.exp(mid - cum) * dtf[:, span], jnp.exp(start + cum)):
            high = value.astype(BF16).astype(F32)
            parts += [high, value - high]
        zero = jnp.zeros((hd, CHUNK), F32)
        feat[span, :] = jnp.concatenate(parts + [zero, zero], 0).T.astype(BF16)
        expo = expo + jnp.where(lane == k, end - mid, 0.0)
        expo = expo + jnp.where(lane == k - 1, mid, 0.0)
        expo = expo + jnp.where(lane == TOTAL_ROW, end, 0.0)
        return start + end, expo

    _, expo = lax.fori_loop(
        0, n_chunk, factors, (jnp.zeros((hd, 1), F32), jnp.zeros((hd, 128), F32))
    )
    fade_t[...] = jnp.where(lane == SKIP_ROW, per_head[:, 2:3], jnp.exp(expo)).T

    def conv(q, start, src):
        cols = pl.ds(start, UNIT)
        taps = w_ref[:, cols].astype(F32)
        window = buf[pl.ds(pl.multiple_of(src * tok, RIM), tok + RIM), place(q)].astype(F32)
        first = RIM - (CONV - 1)
        total = window[first : first + tok] * taps[0:1]
        for k in range(1, CONV):
            total = total + window[first + k : first + k + tok] * taps[k : k + 1]
        total = total + b_ref[:, cols]
        return (total / (1.0 + jnp.exp(-total))).astype(BF16)

    @pl.when(ctx > 0)
    def _():
        for part in range(3):
            rim_arrived(part)

    causal = lax.broadcasted_iota(jnp.int32, (CHUNK, CHUNK), 0) >= lax.broadcasted_iota(
        jnp.int32, (CHUNK, CHUNK), 1
    )

    def projections(src, _):
        unit_arrived(0, src)
        unit_arrived(1, src)
        b_now = conv(0, column(0, me), src)
        c_now = conv(1, column(1, me), src)
        rows = pl.ds(pl.multiple_of(src * tok, tok), tok)
        b_t[:, rows] = b_now.astype(F32).T.astype(BF16)
        c_act[rows, :] = c_now
        for i in range(tok // CHUNK):
            part = slice(i * CHUNK, (i + 1) * CHUNK)
            inner = lax.dot_general(
                c_now[part], b_now[part], (((1,), (1,)), ((), ())), preferred_element_type=F32
            )
            gram[pl.ds(pl.multiple_of(src * tok + i * CHUNK, CHUNK), CHUNK), :] = jnp.where(
                causal, inner, 0.0
            ).astype(BF16)
        return 0

    lax.fori_loop(0, n_head, projections, 0)
    unit_sent(0)
    unit_sent(1)

    row = lax.broadcasted_iota(jnp.int32, (8 * hd, UNIT), 0)
    col = lax.broadcasted_iota(jnp.int32, (8 * hd, UNIT), 1) // HEADDIM

    def spread(p, at):
        head = col + p * per_unit
        hit = jnp.logical_or(row == head + at * hd, row == head + (at + 1) * hd)
        return jnp.where(hit, 1.0, 0.0).astype(BF16)

    def finish(p):
        @pl.when(ctx > 0)
        def _():
            pltpu.make_async_copy(s_in.at[p], s_in.at[p], chain_recv.at[p]).wait()

        @pl.when(ctx < n_ctx - 1)
        def _():
            before = s_in[p].astype(F32)
            s_out[p] = (fade[TOTAL_ROW : TOTAL_ROW + 1, :] * before + state[...]).astype(BF16)
            chain_copy(p).start()

        e_g[...] = spread(p, 4)

        def block(i, _):
            rows = pl.ds(pl.multiple_of(i * tok, tok), tok)
            grown = dot(feat[rows, :], e_g[...])
            late = grown * dot(c_act[rows, :], s_in[p])
            buf[pl.ds(pl.multiple_of(RIM + i * tok, RIM), tok), place(p + 2)] = (
                y_buf[rows, :] + late
            ).astype(BF16)
            return 0

        lax.fori_loop(0, n_head, block, 0)
        out_copy(p).start()

    def piece(p, _):
        unit_sent(p + 2)

        @pl.when(p + AHEAD < pieces)
        def _():
            unit_start(p + AHEAD + 2)

        e_u[...] = spread(p, 0)
        e_v[...] = spread(p, 2)
        expand = jnp.where(row[0:hd] == col[0:hd] + p * per_unit, 1.0, 0.0)
        fade[...] = dot(fade_t[...], expand, lax.Precision.HIGHEST)
        state[...] = jnp.zeros(state.shape, F32)

        def block(src, _):
            unit_arrived(p + 2, src)
            act = conv(p + 2, column(p + 2, me), src).astype(F32)
            rows = pl.ds(pl.multiple_of(src * tok, tok), tok)
            grow = dot(feat[rows, :], e_u[...])
            scaled = (act * dot(feat[rows, :], e_v[...])).astype(BF16)
            for i in range(tok // CHUNK):
                part = slice(i * CHUNK, (i + 1) * CHUNK)
                span = pl.ds(pl.multiple_of(src * tok + i * CHUNK, CHUNK), CHUNK)
                entering = state[...]
                y = dot(gram[span, :], scaled[part]) + dot(c_act[span, :], entering.astype(BF16))
                y_buf[span, :] = (
                    grow[part] * y + fade[SKIP_ROW : SKIP_ROW + 1, :] * act[part]
                )
                added = dot(b_t[:, span], scaled[part])
                k = src * (tok // CHUNK) + i
                state[...] = fade[pl.ds(k, 1), :] * (entering + added)
            return 0

        lax.fori_loop(0, n_head, block, 0)
        finish(p)
        return 0

    lax.fori_loop(0, pieces, piece, 0)

    for d in turns:
        dt_copy(lax.rem(me + d, n_head)).wait_send()

    @pl.when(sends_rim)
    def _():
        for part in range(3):
            for j in range(n_head):
                rim_copy(part, j).wait_send()

    @pl.when(ctx < n_ctx - 1)
    def _():
        for p in range(pieces):
            chain_copy(p).wait_send()

    for p in range(pieces):
        out_copy(p).wait()


def hand_out(result, out_hbm, sem):
    rows = result.shape[0] // PARTS
    copies = [
        pltpu.make_async_copy(
            result.at[pl.ds(i * rows, rows), :], out_hbm.at[pl.ds(i * rows, rows), :], sem.at[i]
        )
        for i in range(PARTS)
    ]
    for copy in copies:
        copy.start()
    for copy in copies:
        copy.wait()


def on_device(conv_input, dt_raw, conv_weight, conv_bias, a_log, dt_bias, d_skip):
    n_ctx, n_head = lax.axis_size("ctx"), lax.axis_size("head")
    tok = conv_input.shape[0]
    length = tok * n_head
    slab = HEADS * HEADDIM // n_head
    hd = HEADS // n_head
    pieces = slab // UNIT
    anywhere = pl.BlockSpec(memory_space=pl.ANY)
    dma = pltpu.SemaphoreType.DMA
    result = pl.pallas_call(
        functools.partial(kernel, n_ctx, n_head),
        out_shape=jax.ShapeDtypeStruct((length, slab), BF16),
        in_specs=[pl.BlockSpec(memory_space=pltpu.HBM)] * 7,
        out_specs=anywhere,
        scratch_shapes=[
            pltpu.VMEM(dt_raw.shape, BF16),
            pltpu.VMEM(conv_weight.shape, BF16),
            pltpu.VMEM((1, conv_bias.shape[0]), F32),
            pltpu.VMEM((1, HEADS), F32),
            pltpu.VMEM((1, HEADS), F32),
            pltpu.VMEM((1, HEADS), F32),
            pltpu.VMEM((RIM + length, slab + 2 * STATE), BF16),
            pltpu.VMEM((HEADS, 8), F32),
            pltpu.VMEM((HEADS, tok), BF16),
            pltpu.VMEM((hd, length), BF16),
            pltpu.VMEM((hd, length), F32),
            pltpu.VMEM((hd, length), F32),
            pltpu.VMEM((STATE, length), BF16),
            pltpu.VMEM((length, STATE), BF16),
            pltpu.VMEM((length, CHUNK), BF16),
            pltpu.VMEM((length, 8 * hd), BF16),
            pltpu.VMEM((128, hd), F32),
            pltpu.VMEM((128, UNIT), F32),
            pltpu.VMEM((8 * hd, UNIT), BF16),
            pltpu.VMEM((8 * hd, UNIT), BF16),
            pltpu.VMEM((8 * hd, UNIT), BF16),
            pltpu.VMEM((length, UNIT), F32),
            pltpu.VMEM((STATE, UNIT), F32),
            pltpu.VMEM((pieces, STATE, UNIT), BF16),
            pltpu.VMEM((pieces, STATE, UNIT), BF16),
            dma((pieces + 2, n_head)),
            dma((pieces + 2, n_head)),
            dma((n_head,)),
            dma((n_head,)),
            dma((3, n_head)),
            dma((3,)),
            dma((pieces,)),
            dma((pieces,)),
            dma((pieces,)),
            dma((6,)),
        ],
        compiler_params=pltpu.CompilerParams(
            collective_id=0, has_side_effects=True, vmem_limit_bytes=40 * 1024 * 1024
        ),
    )(
        conv_input,
        dt_raw,
        conv_weight,
        *(table.reshape(1, -1) for table in (conv_bias, a_log, dt_bias, d_skip)),
    )


    return pl.pallas_call(
        hand_out,
        out_shape=jax.ShapeDtypeStruct((length, slab), BF16),
        in_specs=[anywhere],
        out_specs=pl.BlockSpec(memory_space=pltpu.HBM),
        scratch_shapes=[dma((PARTS,))],
        compiler_params=pltpu.CompilerParams(vmem_limit_bytes=4 * 1024 * 1024),
    )(result)


def solution(mesh):
    placed = (P(("ctx", "head"), None), P(("ctx", "head"), None), P(), P(), P(), P(), P())
    return jax.shard_map(
        on_device, mesh=mesh, in_specs=placed, out_specs=P("ctx", "head"), check_vma=False
    )
```
